256 devices in a mesh: occ: 64 (over z, x_lo, y), slab: 4 (over x_hi, core).
Axes of the slice: x: 4 (x_hi: 2, x_lo: 2; x = x_hi * 2 + x_lo), y: 4, z: 8, core: 2. Of those that a mesh axis runs over, the one named last changes fastest.
Arguments:
- three_centre: bfloat16 [64, 640, 4096], P(None, 'slab', 'occ'), may hold values from -0.75 to 0.75
- eps_occ: float32 [16], replicated, may hold values from -3 to -0.5
- eps_vir: float32 [2560], replicated, may hold values from 0.2 to 4
- block_owner: int32 [64], replicated, may hold values from 0 to 63, each once
- round_order: int32 [2], replicated, may hold values from 0 to 63
Outputs:
- gamma: bfloat16 [64, 640, 4096], P('occ', 'slab')
The draws below stay inside these ranges and needn't reach their ends.
Inputs may be any that keep to these rules, and one draw needn't show every extreme that they name: `block_owner`: each owner position holds a different block.
All inputs are finite; a program needn't handle non-finite values.
Results may differ from the reference program's by a relative error of at most 0.0045.
Values may be sent and summed in bfloat16 or wider, within the bound.
No kernel may reach another device: no remote copies, remote signals or barrier semaphores. Data moves between devices by JAX's collectives and lax.ppermute only.
A program may use at most 64 MiB of HBM per device.

```python
import jax
import jax.numpy as jnp
from jax import lax

V = 2560
NAUX = 4096
ROUNDS = 2
BLOCK_ROWS = 640
OCCUPIED = 16
N_OCC = 64


def block_levels(rng, dims, pieces, smallest, high):
    loudness = 1.0
    for position, blocks in pieces:
        draws = jax.random.uniform(jax.random.fold_in(jax.random.fold_in(rng, 6), position), (blocks,), jnp.float32, smallest / len(pieces), high / len(pieces))
        loudness = loudness * jnp.repeat(jnp.exp(draws), dims[position] // blocks).reshape((-1,) + (1,) * (len(dims) - 1 - position))
    return loudness


def scatter_about(stream_key, extent, deviation, bound, pieces=(), held_as=jnp.bfloat16):
    array = deviation * jax.random.normal(stream_key, extent, jnp.float32)
    if pieces:
        array = array * block_levels(stream_key, extent, pieces, -0.22, 0.18)
    return jnp.clip(array, -bound, bound).astype(held_as)


def setup_inputs(seed: int = 0) -> dict:
    arg_keys = jax.random.split(jax.random.key(seed), 6)
    three_centre = scatter_about(arg_keys[0], (N_OCC, BLOCK_ROWS, NAUX), 0.125, 0.75, ((1, 4), (2, 64)))
    eps_occ = jnp.clip(jax.random.uniform(arg_keys[1], (OCCUPIED,), jnp.float32, -3.0, -0.5), -3.0, -0.5)
    eps_vir = jnp.clip(jax.random.uniform(arg_keys[2], (V,), jnp.float32, 0.2, 4.0), 0.2, 4.0)
    block_owner = jax.random.permutation(arg_keys[3], N_OCC).astype(jnp.int32)
    round_order = jax.random.randint(arg_keys[4], (ROUNDS,), 0, N_OCC).astype(jnp.int32)
    return dict(three_centre=three_centre, eps_occ=eps_occ, eps_vir=eps_vir, block_owner=block_owner, round_order=round_order)


def pair_gaps(owner_slot, block_owner, eps_occ, eps_vir):
    first_pair = block_owner[owner_slot] * BLOCK_ROWS
    pair_ids = first_pair + jnp.arange(BLOCK_ROWS, dtype=jnp.int32)
    return eps_occ[pair_ids // V] - eps_vir[pair_ids % V]


def reference(three_centre, eps_occ, eps_vir, block_owner, round_order):
    slots = jnp.arange(N_OCC, dtype=jnp.int32)
    gaps_all = jax.vmap(lambda owner_slot: pair_gaps(owner_slot, block_owner, eps_occ, eps_vir))(slots)

    def one_slot(operands):
        my_block, my_gaps = operands
        gamma_sum = jnp.zeros((BLOCK_ROWS, NAUX), jnp.float32)
        for round_step in range(ROUNDS):
            root_slot = round_order[round_step]
            sent_block = three_centre[root_slot]
            intersection = lax.dot_general(my_block, sent_block, (((1,), (1,)), ((), ())), preferred_element_type=jnp.float32)
            denominator = my_gaps[:, None] + gaps_all[root_slot][None, :]
            amplitude = (intersection / denominator).astype(jnp.bfloat16)
            gamma_sum = gamma_sum + jnp.dot(amplitude, sent_block, preferred_element_type=jnp.float32)
        return gamma_sum.astype(jnp.bfloat16)

    return lax.map(one_slot, (three_centre, gaps_all))
```

```python
import functools

import jax
import jax.numpy as jnp
from jax import lax
from jax.experimental import pallas as pl
from jax.experimental.pallas import tpu as pltpu
from jax.sharding import PartitionSpec as P

ROUNDS = 2
NZ, NX, NY, NC = 8, 4, 4, 2
XY = 8
COLS = 64
ROWS = 160
TAIL = ROWS - 128
PACKED = COLS + COLS * TAIL // 128
GROUPS = 128 // TAIL
GROUP_COLS = COLS // GROUPS
BOTH = ("occ", "slab")
VMEM_LIMIT = 48 * 1024 * 1024


def index(z, x, y, core):
    return ((z % NZ) * XY + (x % 2) * NY + y % NY) * 4 + (x % NX) // 2 * 2 + core


def fetch(block, dz=0, dx=0, dy=0, swap=0):
    pairs = [
        (index(z + dz, x + dx, y + dy, core ^ swap), index(z, x, y, core))
        for z in range(NZ) for x in range(NX) for y in range(NY) for core in range(NC)
    ]
    return lax.ppermute(block, BOTH, pairs)


def pack_piece(piece):
    tail = piece[:, 128:]
    tail = [tail[g * GROUP_COLS:(g + 1) * GROUP_COLS] for g in range(GROUPS)]
    return piece[:, :128], jnp.concatenate(tail, axis=1)


def pack_rounds_kernel(order, piece, out):
    main, tail = pack_piece(piece[0])
    out[0, :COLS] = main
    out[0, COLS:] = tail


def pack_all_kernel(pieces, out):
    for b in range(pieces.shape[0]):
        main, tail = pack_piece(pieces[b])
        out[b, :COLS] = main
        out[b, COLS:] = tail


def pack_rounds(columns, round_order):
    return pl.pallas_call(
        pack_rounds_kernel,
        grid_spec=pltpu.PrefetchScalarGridSpec(
            num_scalar_prefetch=1,
            grid=(ROUNDS,),
            in_specs=[pl.BlockSpec((1, COLS, ROWS), lambda k, order: (order[k], 0, 0))],
            out_specs=pl.BlockSpec((1, PACKED, 128), lambda k, order: (k, 0, 0)),
        ),
        out_shape=jax.ShapeDtypeStruct((ROUNDS, PACKED, 128), jnp.bfloat16),
    )(round_order, columns)


def pack_all(columns):
    blocks = columns.shape[0]
    step = 16
    return pl.pallas_call(
        pack_all_kernel,
        grid=(blocks // step,),
        in_specs=[pl.BlockSpec((step, COLS, ROWS), lambda b: (b, 0, 0))],
        out_specs=pl.BlockSpec((step, PACKED, 128), lambda b: (b, 0, 0)),
        out_shape=jax.ShapeDtypeStruct((blocks, PACKED, 128), jnp.bfloat16),
    )(columns)


def rows_kernel(place, packed, out):
    for dz in range(NZ):
        plane = lax.rem(place[0] + dz, NZ)
        block = packed[pl.ds(plane * XY, XY)]
        span = pl.ds(dz * XY * COLS, XY * COLS)
        out[:128, span] = block[:, :COLS].reshape(XY * COLS, 128).T
        tail = block[:, COLS:].astype(jnp.float32).reshape(XY * GROUP_COLS, 128)
        groups = [tail if g == 0 else pltpu.roll(tail, 128 - TAIL * g, 1) for g in range(GROUPS)]
        groups = [v.reshape(XY, 1, GROUP_COLS, 128) for v in groups]
        tail = jnp.concatenate(groups, axis=1).reshape(XY * COLS, 128)
        out[128:, span] = tail.T[:TAIL].astype(jnp.bfloat16)


def unpack_rows(place, packed):
    return pl.pallas_call(
        rows_kernel,
        in_specs=[pl.BlockSpec(memory_space=pltpu.SMEM), pl.BlockSpec(memory_space=pltpu.VMEM)],
        out_specs=pl.BlockSpec(memory_space=pltpu.VMEM),
        out_shape=jax.ShapeDtypeStruct((ROWS, NZ * XY * COLS), jnp.bfloat16),
        compiler_params=pltpu.CompilerParams(vmem_limit_bytes=VMEM_LIMIT),
    )(place, packed)


def gamma_kernel(layout, place, rows, left_gap, right_gap, *rest):
    count = len(layout)
    pieces, (out, weights, tails, amplitude, sems) = rest[:count], rest[count:]
    my_x, my_y, my_core = place[1], place[2], place[3]
    copies = []
    for piece, (k, along, dx, dy, swap, first) in zip(pieces, layout):
        for step in range(piece.shape[0]):
            x = lax.rem(my_x + dx + (first + step if along == "x" else 0), NX)
            y = lax.rem(my_y + dy + (first + step if along == "y" else 0), NY)
            core = 1 - my_core if swap else my_core
            spot = lax.rem(x, 2) * NY + y
            slab = lax.div(x, 2) * NC + core
            copies.append(pltpu.make_async_copy(
                piece.at[step, :, pl.ds(0, COLS)], weights.at[k * 4 + slab, :, spot], sems.at[0]))
            copies.append(pltpu.make_async_copy(
                piece.at[step, :, pl.ds(COLS, PACKED - COLS)], tails.at[k, slab, :, spot], sems.at[0]))
    for copy in copies:
        copy.start()
    for copy in copies:
        copy.wait()
    depth = NZ * XY * COLS
    source = lax.broadcasted_iota(jnp.int32, (4 * 128, 4 * 128), 0)
    target = lax.broadcasted_iota(jnp.int32, (4 * 128, 4 * 128), 1)
    moved = (source // TAIL % GROUPS) * 128 + source // 128 * TAIL + source % TAIL
    shuffle = jnp.where(moved == target, 1.0, 0.0).astype(jnp.bfloat16)
    for k in range(ROUNDS):
        lanes = [tails[k, s].reshape(NZ * XY * GROUP_COLS, 128) for s in range(4)]
        swapped = jnp.dot(jnp.concatenate(lanes, axis=1), shuffle, preferred_element_type=jnp.float32)
        swapped = swapped.astype(jnp.bfloat16)
        for g in range(GROUPS):
            part = swapped[:, g * 128:(g + 1) * 128].reshape(NZ, XY, GROUP_COLS, 128)
            weights[4 * ROUNDS + k, :, :, g * GROUP_COLS:(g + 1) * GROUP_COLS] = part
    tiles = 5 * ROUNDS
    for t in range(0, tiles, 2):
        pair = [weights[u].reshape(depth, 128) for u in (t, t + 1)]
        span = slice(t * 128, (t + 2) * 128)
        product = jnp.dot(rows[...], jnp.concatenate(pair, axis=1), preferred_element_type=jnp.float32)
        amplitude[:, span] = (product / (left_gap[...] + right_gap[:, span])).astype(jnp.bfloat16)
    for dz in range(NZ):
        plane = lax.rem(place[0] + dz, NZ)
        part = [weights[u, dz].reshape(XY * COLS, 128) for u in range(tiles)]
        part = lax.dot_general(
            amplitude[...], jnp.concatenate(part, axis=1), (((1,), (1,)), ((), ())),
            preferred_element_type=jnp.float32)
        out[:, pl.ds(pl.multiple_of(plane * (XY * COLS), XY * COLS), XY * COLS)] = part.astype(jnp.bfloat16)


def gamma(place, rows, left_gap, right_gap, pieces, layout):
    vmem = pl.BlockSpec(memory_space=pltpu.VMEM)
    return pl.pallas_call(
        functools.partial(gamma_kernel, layout),
        in_specs=[pl.BlockSpec(memory_space=pltpu.SMEM)] + [vmem] * 3
        + [pl.BlockSpec(memory_space=pl.ANY)] * len(pieces),
        out_specs=vmem,
        out_shape=jax.ShapeDtypeStruct((ROWS, NZ * XY * COLS), jnp.bfloat16),
        scratch_shapes=[
            pltpu.VMEM((5 * ROUNDS, NZ, XY, COLS, 128), jnp.bfloat16),
            pltpu.VMEM((ROUNDS, 4, NZ, XY, GROUP_COLS, 128), jnp.bfloat16),
            pltpu.VMEM((ROWS, 5 * ROUNDS * 128), jnp.bfloat16),
            pltpu.SemaphoreType.DMA((1,)),
        ],
        compiler_params=pltpu.CompilerParams(vmem_limit_bytes=VMEM_LIMIT),
    )(place, rows, left_gap, right_gap, *pieces)


def on_device(three_centre, eps_occ, eps_vir, block_owner, round_order):
    columns = jnp.swapaxes(three_centre, 1, 2)
    vir_count = eps_vir.shape[0]
    block_span = 4 * ROWS

    occ, slab = lax.axis_index("occ"), lax.axis_index("slab")
    place = jnp.stack([occ // XY, slab // 2 * 2 + occ // NY % 2, occ % NY, slab % 2]).astype(jnp.int32)

    own = pack_rounds(columns, round_order)
    pair = jnp.stack([own, fetch(own, dz=1)])
    far = [fetch(pair, dz=d) for d in (2, 4, 6)]
    line = jnp.concatenate([pair] + far)

    packed = pack_all(columns)
    packed = lax.all_to_all(packed, "occ", split_axis=0, concat_axis=0, tiled=True)

    pieces, layout = [], []

    def keep(array, *where):
        pieces.append(array)
        layout.append((where[0], where[1], where[2], where[3], 0, where[4]))
        pieces.append(fetch(array, swap=1))
        layout.append((where[0], where[1], where[2], where[3], 1, where[4]))

    for k, first, second in ((0, "y", "x"), (1, "x", "y")):
        mine = line[:, k]
        d1, d2 = "d" + first, "d" + second

        def spot(d):
            return (d, 0) if second == "x" else (0, d)

        face = jnp.stack([mine] + [fetch(mine, **{d1: d}) for d in (1, 2, 3)])
        keep(face, k, first, *spot(0), 0)
        ahead, behind = fetch(face, **{d2: 1}), fetch(face, **{d2: 3})
        keep(ahead, k, first, *spot(1), 0)
        keep(behind, k, first, *spot(3), 0)
        keep(fetch(ahead[:2], **{d2: 1}), k, first, *spot(2), 0)
        keep(fetch(behind[2:], **{d2: 3}), k, first, *spot(2), 2)

    def energies(owner_slot, row_offset, span_rows):
        first_pair = block_owner[owner_slot] * block_span + row_offset
        occ_level = lax.dynamic_slice_in_dim(eps_occ, first_pair // vir_count, 1)
        vir_level = lax.dynamic_slice_in_dim(eps_vir, first_pair % vir_count, span_rows)
        return occ_level - vir_level

    left_gap = energies(occ, slab * ROWS, ROWS)[:, None]
    right = jnp.stack([energies(round_order[k], 0, block_span) for k in range(ROUNDS)])
    right = right.reshape(ROUNDS, 4, ROWS)
    right_gap = jnp.concatenate([right[:, :, :128].reshape(1, -1), right[:, :, 128:].reshape(1, -1)], axis=1)

    rows = unpack_rows(place, packed)
    return gamma(place, rows, left_gap, right_gap, pieces, tuple(layout))[None]


def solution(mesh):
    in_specs = (P(None, "slab", "occ"), P(), P(), P(), P())
    out_specs = P("occ", "slab", None)
    return jax.shard_map(
        on_device, mesh=mesh, in_specs=in_specs, out_specs=out_specs, check_vma=False
    )
```

```python
import functools

import jax
import jax.numpy as jnp
from jax import lax
from jax.experimental import pallas as pl
from jax.experimental.pallas import tpu as pltpu
from jax.sharding import PartitionSpec as P

ROUNDS = 2
NZ, NX, NY, NC = 8, 4, 4, 2
XY = 8
COLS = 64
ROWS = 160
TAIL = ROWS - 128
PACKED = COLS + COLS * TAIL // 128
GROUPS = 128 // TAIL
GROUP_COLS = COLS // GROUPS
BOTH = ("occ", "slab")
LINE = 2 * COLS + COLS // 2
CHUNKS = 2
VMEM_LIMIT = 20 * 1024 * 1024


def index(z, x, y, core):
    return ((z % NZ) * XY + (x % 2) * NY + y % NY) * 4 + (x % NX) // 2 * 2 + core


def fetch(block, dz=0, first=0, second=0, swap=0):
    pairs = []
    for z in range(NZ):
        for x in range(NX):
            for y in range(NY):
                for core in range(NC):
                    dx, dy = (first, second) if core else (second, first)
                    pairs.append((index(z + dz, x + dx, y + dy, core ^ swap), index(z, x, y, core)))
    return lax.ppermute(block, BOTH, pairs)


def position():
    occ, slab = lax.axis_index("occ"), lax.axis_index("slab")
    return lax.div(occ, XY), lax.div(slab, 2) * 2 + lax.rem(lax.div(occ, NY), 2), lax.rem(occ, NY), lax.rem(slab, 2)


def pack_kernel(order, pieces, first, second, line, out):
    @pl.when(pl.program_id(0) == 0)
    def _():
        rounds = first[0], second[0]
        line[:COLS] = rounds[0][:, :128]
        line[COLS:2 * COLS] = rounds[1][:, :128]
        half = COLS // 2
        line[2 * COLS:] = jnp.concatenate([p[h:h + half, 128:] for h in (0, half) for p in rounds], axis=1)

    step = pieces.shape[0]
    for b in range(step):
        piece = pieces[b]
        z, spot = pl.program_id(0) * (step // XY) + b // XY, b % XY
        out[spot, z, :COLS] = piece[:, :128]
        tail = [piece[g * GROUP_COLS:(g + 1) * GROUP_COLS, 128:] for g in range(GROUPS)]
        out[spot, z, COLS:] = jnp.concatenate(tail, axis=1)


def pack(columns, round_order):
    blocks = columns.shape[0]
    step = 32
    return pl.pallas_call(
        pack_kernel,
        grid_spec=pltpu.PrefetchScalarGridSpec(
            num_scalar_prefetch=1,
            grid=(blocks // step,),
            in_specs=[
                pl.BlockSpec((step, COLS, ROWS), lambda i, order: (i, 0, 0)),
                pl.BlockSpec((1, COLS, ROWS), lambda i, order: (order[0], 0, 0)),
                pl.BlockSpec((1, COLS, ROWS), lambda i, order: (order[1], 0, 0)),
            ],
            out_specs=[
                pl.BlockSpec((LINE, 128), lambda i, order: (0, 0)),
                pl.BlockSpec((NZ, XY, PACKED, 128), lambda i, order: (0, 0, 0, 0)),
            ],
        ),
        out_shape=[
            jax.ShapeDtypeStruct((LINE, 128), jnp.bfloat16),
            jax.ShapeDtypeStruct((NZ, XY, PACKED, 128), jnp.bfloat16),
        ],
        compiler_params=pltpu.CompilerParams(vmem_limit_bytes=VMEM_LIMIT),
    )(round_order, columns, columns, columns)


def exchange(packed, planes):
    groups = [[m * XY + o if planes else o * XY + m for m in range(8)] for o in range(8)]
    return lax.all_to_all(packed, "occ", split_axis=0, concat_axis=0, axis_index_groups=groups, tiled=True)


def rows_kernel(owner, order, eps_occ, eps_vir, packed, out, left_gap, right_gap):
    span = 4 * ROWS
    vir_blocks = eps_vir.shape[1] // span

    def energies(slot):
        block = owner[slot]
        start = pl.multiple_of(lax.rem(block, vir_blocks) * span, 128)
        return eps_occ[lax.div(block, vir_blocks)] - eps_vir[:, pl.ds(start, span)]

    mine = energies(lax.axis_index("occ"))
    left = mine[:, :ROWS]
    for s in range(1, 4):
        left = jnp.where(lax.axis_index("slab") == s, mine[:, s * ROWS:(s + 1) * ROWS], left)
    left = jnp.concatenate([left, jnp.zeros((1, 256 - ROWS), jnp.float32)], axis=1)
    left_gap[...] = jnp.broadcast_to(left, (128, 256)).T[:ROWS]
    theirs = [energies(order[k]) for k in range(ROUNDS)]
    for s in range(4):
        right_gap[s] = jnp.concatenate([t[:, s * ROWS:s * ROWS + 128] for t in theirs], axis=1)
    tails = [t[:, s * ROWS + 128:(s + 1) * ROWS] for s in range(4) for t in theirs]
    right_gap[4] = jnp.concatenate(tails, axis=1)

    my_z = position()[0]
    for dz in range(NZ):
        plane = lax.rem(my_z + dz, NZ)
        cols = pl.ds(dz * XY * COLS, XY * COLS)
        block = packed[plane]
        out[:128, cols] = block[:, :COLS].reshape(XY * COLS, 128).T
        tail = block[:, COLS:].astype(jnp.float32).reshape(XY * GROUP_COLS, 128)
        groups = [tail if g == 0 else pltpu.roll(tail, 128 - TAIL * g, 1) for g in range(GROUPS)]
        groups = [v.reshape(XY, 1, GROUP_COLS, 128) for v in groups]
        tail = jnp.concatenate(groups, axis=1).reshape(XY * COLS, 128)
        out[128:, cols] = tail.T[:TAIL].astype(jnp.bfloat16)


def unpack_rows(block_owner, round_order, eps_occ, eps_vir, packed):
    smem = pl.BlockSpec(memory_space=pltpu.SMEM)
    vmem = pl.BlockSpec(memory_space=pltpu.VMEM)
    return pl.pallas_call(
        rows_kernel,
        in_specs=[smem] * 3 + [vmem] * 2,
        out_specs=[vmem] * 3,
        out_shape=[
            jax.ShapeDtypeStruct((ROWS, NZ * XY * COLS), jnp.bfloat16),
            jax.ShapeDtypeStruct((ROWS, 128), jnp.float32),
            jax.ShapeDtypeStruct((5, 1, 256), jnp.float32),
        ],
        compiler_params=pltpu.CompilerParams(vmem_limit_bytes=VMEM_LIMIT),
    )(block_owner, round_order, eps_occ, eps_vir[None], packed)


def gamma_kernel(layout, rows, left_gap, right_gap, *rest):
    count = len(layout)
    pieces, (out, weights, tails, product, amplitude, sems) = rest[:count], rest[count:]
    my_z, my_x, my_y, my_core = position()
    planes = NZ // CHUNKS
    plane_cols = XY * COLS

    def copy(chunk, piece, step, second, swap, begin):
        core = 1 - my_core if swap else my_core
        first = begin + step
        x = lax.rem(my_x + jnp.where(core == 0, second, first), NX)
        y = lax.rem(my_y + jnp.where(core == 0, first, second), NY)
        span = pl.ds(chunk * planes, planes)
        return pltpu.make_async_copy(
            piece.at[step, span], weights.at[lax.div(x, 2) * NC + core, span, lax.rem(x, 2) * NY + y],
            sems.at[chunk])

    copies = [
        [copy(c, piece, step, *where) for piece, where in zip(pieces, layout) for step in range(piece.shape[0])]
        for c in range(CHUNKS)
    ]
    for c in range(CHUNKS):
        for one in copies[c]:
            one.start()

    half = COLS // 2
    for c in range(CHUNKS):
        for one in copies[c]:
            one.wait()
        span = slice(c * planes, (c + 1) * planes)
        for h in range(2):
            low = weights[2 * h, span, :, 2 * COLS:]
            high = weights[2 * h + 1, span, :, 2 * COLS:]
            tails[h, span, :, :half] = jnp.concatenate([low[..., :64], high[..., :64]], axis=-1)
            tails[h, span, :, half:] = jnp.concatenate([low[..., 64:], high[..., 64:]], axis=-1)
        mine = rows[:, c * planes * plane_cols:(c + 1) * planes * plane_cols]
        for p in range(5):
            if p < 4:
                pair = [weights[p, span, :, k * COLS:(k + 1) * COLS] for k in range(ROUNDS)]
            else:
                pair = [tails[h, span] for h in range(2)]
            pair = [v.reshape(planes * plane_cols, 128) for v in pair]
            part = jnp.dot(mine, jnp.concatenate(pair, axis=1), preferred_element_type=jnp.float32)
            if c > 0:
                part += product[p]
            if c < CHUNKS - 1:
                product[p] = part
            else:
                left = jnp.concatenate([left_gap[...]] * 2, axis=1)
                amplitude[:, p * 256:(p + 1) * 256] = (part / (left + right_gap[p])).astype(jnp.bfloat16)
    for dz in range(NZ):
        plane = lax.rem(my_z + dz, NZ)
        part = [weights[p, dz, :, k * COLS:(k + 1) * COLS] for p in range(4) for k in range(ROUNDS)]
        part += [tails[h, dz] for h in range(2)]
        part = jnp.concatenate([v.reshape(plane_cols, 128) for v in part], axis=1)
        part = lax.dot_general(
            amplitude[...], part, (((1,), (1,)), ((), ())), preferred_element_type=jnp.float32)
        out[:, pl.ds(pl.multiple_of(plane * plane_cols, plane_cols), plane_cols)] = part.astype(jnp.bfloat16)


def gamma(rows, left_gap, right_gap, pieces, layout):
    vmem = pl.BlockSpec(memory_space=pltpu.VMEM)
    return pl.pallas_call(
        functools.partial(gamma_kernel, layout),
        in_specs=[vmem] * 3
        + [pl.BlockSpec(memory_space=pl.ANY)] * len(pieces),
        out_specs=vmem,
        out_shape=jax.ShapeDtypeStruct((ROWS, NZ * XY * COLS), jnp.bfloat16),
        scratch_shapes=[
            pltpu.VMEM((4, NZ, XY, LINE, 128), jnp.bfloat16),
            pltpu.VMEM((2, NZ, XY, COLS, 128), jnp.bfloat16),
            pltpu.VMEM((5, ROWS, 256), jnp.float32),
            pltpu.VMEM((ROWS, 5 * 256), jnp.bfloat16),
            pltpu.SemaphoreType.DMA((CHUNKS,)),
        ],
        compiler_params=pltpu.CompilerParams(vmem_limit_bytes=VMEM_LIMIT),
    )(rows, left_gap, right_gap, *pieces)


def on_device(three_centre, eps_occ, eps_vir, block_owner, round_order):
    columns = jnp.swapaxes(three_centre, 1, 2)

    own, packed = pack(columns, round_order)
    pair = jnp.stack([own, fetch(own, dz=1)])
    far = [fetch(pair, dz=d) for d in (2, 4, 6)]
    line = jnp.concatenate([pair] + far)

    packed = exchange(packed, False)
    packed = exchange(jnp.swapaxes(packed, 0, 1), True)

    pieces, layout = [], []

    def keep(array, second, begin):
        pieces.extend([array, fetch(array, swap=1)])
        layout.extend([(second, 0, begin), (second, 1, begin)])

    low = jnp.stack([line, fetch(line, first=1)])
    high = jnp.stack([fetch(line, first=2), fetch(line, first=3)])
    keep(low, 0, 0)
    keep(high, 0, 2)
    ahead_low, behind_high = fetch(low, second=1), fetch(high, second=3)
    ahead_high, behind_low = fetch(high, second=1), fetch(low, second=3)
    keep(ahead_low, 1, 0)
    keep(behind_high, 3, 2)
    keep(ahead_high, 1, 2)
    keep(behind_low, 3, 0)
    keep(fetch(ahead_low, second=1), 2, 0)
    keep(fetch(behind_high, second=3), 2, 2)

    rows, left_gap, right_gap = unpack_rows(block_owner, round_order, eps_occ, eps_vir, packed)
    return gamma(rows, left_gap, right_gap, pieces, tuple(layout))[None]


def solution(mesh):
    in_specs = (P(None, "slab", "occ"), P(), P(), P(), P())
    out_specs = P("occ", "slab", None)
    return jax.shard_map(
        on_device, mesh=mesh, in_specs=in_specs, out_specs=out_specs, check_vma=False
    )
```

```python
import functools

import jax
import jax.numpy as jnp
from jax import lax
from jax.experimental import pallas as pl
from jax.experimental.pallas import tpu as pltpu
from jax.sharding import PartitionSpec as P

ROUNDS = 2
NZ, NX, NY, NC = 8, 4, 4, 2
XY = 8
COLS = 64
ROWS = 160
TAIL = ROWS - 128
PACKED = COLS + COLS * TAIL // 128
GROUPS = 128 // TAIL
GROUP_COLS = COLS // GROUPS
BOTH = ("occ", "slab")
LINE = 2 * COLS + COLS // 2
VMEM_LIMIT = 20 * 1024 * 1024


def index(z, x, y, core):
    return ((z % NZ) * XY + (x % 2) * NY + y % NY) * 4 + (x % NX) // 2 * 2 + core


def fetch(block, dz=0, first=0, second=0, swap=0):
    pairs = []
    for z in range(NZ):
        for x in range(NX):
            for y in range(NY):
                for core in range(NC):
                    dx, dy = (first, second) if core else (second, first)
                    pairs.append((index(z + dz, x + dx, y + dy, core ^ swap), index(z, x, y, core)))
    return lax.ppermute(block, BOTH, pairs)


def position():
    occ, slab = lax.axis_index("occ"), lax.axis_index("slab")
    return lax.div(occ, XY), lax.div(slab, 2) * 2 + lax.rem(lax.div(occ, NY), 2), lax.rem(occ, NY), lax.rem(slab, 2)


def line_kernel(order, columns, out, rounds, sems):
    copies = [
        pltpu.make_async_copy(columns.at[order[k]], rounds.at[k], sems.at[k]) for k in range(ROUNDS)]
    for copy in copies:
        copy.start()
    for copy in copies:
        copy.wait()
    for k in range(ROUNDS):
        out[k * COLS:(k + 1) * COLS] = rounds[k, :, :128]
    half = COLS // 2
    tail = [rounds[k, h:h + half, 128:] for h in (0, half) for k in range(ROUNDS)]
    out[2 * COLS:] = jnp.concatenate(tail, axis=1)


def pack_line(columns, round_order):
    return pl.pallas_call(
        line_kernel,
        in_specs=[pl.BlockSpec(memory_space=pltpu.SMEM), pl.BlockSpec(memory_space=pltpu.HBM)],
        out_specs=pl.BlockSpec(memory_space=pltpu.VMEM),
        out_shape=jax.ShapeDtypeStruct((LINE, 128), jnp.bfloat16),
        scratch_shapes=[pltpu.VMEM((ROUNDS, COLS, ROWS), jnp.bfloat16), pltpu.SemaphoreType.DMA((ROUNDS,))],
    )(round_order, columns)


def pack_kernel(pieces, out):
    step = pieces.shape[0]
    for b in range(step):
        piece = pieces[b]
        z, spot = pl.program_id(0) * (step // XY) + b // XY, b % XY
        out[spot, z, :COLS] = piece[:, :128]
        tail = [piece[g * GROUP_COLS:(g + 1) * GROUP_COLS, 128:] for g in range(GROUPS)]
        out[spot, z, COLS:] = jnp.concatenate(tail, axis=1)


def pack(columns):
    blocks = columns.shape[0]
    step = 32
    return pl.pallas_call(
        pack_kernel,
        grid=(blocks // step,),
        in_specs=[pl.BlockSpec((step, COLS, ROWS), lambda i: (i, 0, 0))],
        out_specs=pl.BlockSpec((XY, NZ, PACKED, 128), lambda i: (0, 0, 0, 0)),
        out_shape=jax.ShapeDtypeStruct((XY, NZ, PACKED, 128), jnp.bfloat16),
        compiler_params=pltpu.CompilerParams(vmem_limit_bytes=VMEM_LIMIT),
    )(columns)


def exchange(packed, planes):
    groups = [[m * XY + o if planes else o * XY + m for m in range(8)] for o in range(8)]
    return lax.all_to_all(packed, "occ", split_axis=0, concat_axis=0, axis_index_groups=groups, tiled=True)


def gamma_kernel(layout, owner, order, eps_occ, eps_vir, packed, *refs):
    pieces, (out, weights, tails, block_ref, rows, right, amplitude, result, load_sems, store_sem) = (
        refs[:len(layout)], refs[len(layout):])
    my_z, my_x, my_y, my_core = position()
    fetch_block = pltpu.make_async_copy(packed, block_ref, load_sems.at[NC])
    fetch_block.start()
    copies = [[], []]
    for swap in range(NC):
        for piece, (second, swapped, first) in zip(pieces, layout):
            if swapped == swap:
                place = weights.at[swap, second, pl.ds(first, piece.shape[0])]
                copies[swap].append(pltpu.make_async_copy(piece, place, load_sems.at[swap]))
    for copy in copies[0] + copies[1]:
        copy.start()

    def line_of(swap, x_hi, spot):
        core = 1 - my_core if swap else my_core
        dx = lax.rem(x_hi * 2 + spot // NY + NX - my_x, NX)
        dy = lax.rem(spot % NY + NY - my_y, NY)
        return weights.at[swap, jnp.where(core == 0, dx, dy), jnp.where(core == 0, dy, dx)]

    span = 4 * ROWS
    vir_blocks = eps_vir.shape[1] // span

    def energies(slot):
        block = owner[slot]
        start = pl.multiple_of(lax.rem(block, vir_blocks) * span, 128)
        return eps_occ[lax.div(block, vir_blocks)] - eps_vir[:, pl.ds(start, span)]

    mine = energies(lax.axis_index("occ"))
    left = mine[:, :ROWS]
    for s in range(1, 4):
        left = jnp.where(lax.axis_index("slab") == s, mine[:, s * ROWS:(s + 1) * ROWS], left)
    left = jnp.concatenate([left, jnp.zeros((1, 256 - ROWS), jnp.float32)], axis=1)
    left = jnp.broadcast_to(left, (256, 256)).T[:ROWS]
    theirs = [energies(order[k]) for k in range(ROUNDS)]
    for s in range(4):
        right[s] = jnp.concatenate([t[:, s * ROWS:s * ROWS + 128] for t in theirs], axis=1)
    right[4] = jnp.concatenate(
        [t[:, s * ROWS + 128:(s + 1) * ROWS] for s in range(4) for t in theirs], axis=1)

    plane_cols = XY * COLS
    fetch_block.wait()
    for dz in range(NZ):
        cols = slice(dz * plane_cols, (dz + 1) * plane_cols)
        block = block_ref[lax.rem(my_z + dz, NZ)]
        rows[:128, cols] = block[:, :COLS].reshape(plane_cols, 128).T
        tail = block[:, COLS:].astype(jnp.float32).reshape(XY * GROUP_COLS, 128)
        groups = [tail if g == 0 else pltpu.roll(tail, 128 - TAIL * g, 1) for g in range(GROUPS)]
        groups = [v.reshape(XY, 1, GROUP_COLS, 128) for v in groups]
        tail = jnp.concatenate(groups, axis=1).reshape(plane_cols, 128)
        rows[128:, cols] = tail.T[:TAIL].astype(jnp.bfloat16)

    def contract(p, pair):
        part = jnp.dot(rows[...], jnp.concatenate(pair, axis=1), preferred_element_type=jnp.float32)
        amplitude[p] = (part / (left + right[p])).astype(jnp.bfloat16)

    def slab_cols(lines, k, planes):
        return jnp.concatenate([v[z, k * COLS:(k + 1) * COLS] for z in planes for v in lines], axis=0)

    for swap in range(NC):
        for copy in copies[swap]:
            copy.wait()
        for h in range(2):
            lines = [line_of(swap, h, spot) for spot in range(XY)]
            p = 2 * h + (1 - my_core if swap else my_core)
            contract(p, [slab_cols(lines, k, range(NZ)) for k in range(ROUNDS)])
    half = COLS // 2
    for h in range(2):
        for spot in range(XY):
            mine, other = line_of(0, h, spot), line_of(1, h, spot)
            for z in range(NZ):
                mine_tail, other_tail = mine[z, 2 * COLS:], other[z, 2 * COLS:]
                low = jnp.where(my_core == 0, mine_tail, other_tail)
                high = jnp.where(my_core == 0, other_tail, mine_tail)
                tails[h, z, spot, :half] = jnp.concatenate([low[:, :64], high[:, :64]], axis=1)
                tails[h, z, spot, half:] = jnp.concatenate([low[:, 64:], high[:, 64:]], axis=1)
    contract(4, [tails[h].reshape(NZ * plane_cols, 128) for h in range(2)])

    slabs = [2 * h + (1 - my_core if swap else my_core) for swap in range(NC) for h in range(2)] + [4]
    turned = jnp.concatenate([amplitude[p] for p in slabs], axis=1).T
    lines = [[line_of(swap, h, spot) for spot in range(XY)] for swap in range(NC) for h in range(2)]
    stores = []
    for dz in range(NZ):
        part = [slab_cols(slab, k, [dz]) for slab in lines for k in range(ROUNDS)]
        part += [tails[h, dz].reshape(plane_cols, 128) for h in range(2)]
        part = jnp.concatenate(part, axis=1)
        part = jnp.dot(part, turned, preferred_element_type=jnp.float32)
        result[dz] = part.astype(jnp.bfloat16).T
        start = pl.multiple_of(lax.rem(my_z + dz, NZ) * plane_cols, plane_cols)
        stores.append(pltpu.make_async_copy(result.at[dz], out.at[:, pl.ds(start, plane_cols)], store_sem))
        stores[-1].start()
    for store in stores:
        store.wait()


def gamma(block_owner, round_order, eps_occ, vir_row, packed, pieces, layout):
    smem = pl.BlockSpec(memory_space=pltpu.SMEM)
    vmem = pl.BlockSpec(memory_space=pltpu.VMEM)
    return pl.pallas_call(
        functools.partial(gamma_kernel, layout),
        in_specs=[smem] * 3 + [vmem] + [pl.BlockSpec(memory_space=pl.ANY)] * (1 + len(pieces)),
        out_specs=pl.BlockSpec(memory_space=pltpu.HBM),
        out_shape=jax.ShapeDtypeStruct((ROWS, NZ * XY * COLS), jnp.bfloat16),
        scratch_shapes=[
            pltpu.VMEM((NC, 4, 4, NZ, LINE, 128), jnp.bfloat16),
            pltpu.VMEM((2, NZ, XY, COLS, 128), jnp.bfloat16),
            pltpu.VMEM((NZ, XY, PACKED, 128), jnp.bfloat16),
            pltpu.VMEM((ROWS, NZ * XY * COLS), jnp.bfloat16),
            pltpu.VMEM((5, 1, 256), jnp.float32),
            pltpu.VMEM((5, ROWS, 256), jnp.bfloat16),
            pltpu.VMEM((NZ, ROWS, XY * COLS), jnp.bfloat16),
            pltpu.SemaphoreType.DMA((NC + 1,)),
            pltpu.SemaphoreType.DMA,
        ],
        compiler_params=pltpu.CompilerParams(vmem_limit_bytes=60 * 1024 * 1024),
    )(block_owner, round_order, eps_occ, vir_row, packed, *pieces)


def on_device(three_centre, eps_occ, eps_vir, block_owner, round_order):
    columns = jnp.swapaxes(three_centre, 1, 2)

    own = pack_line(columns, round_order)
    above = fetch(own, dz=1)
    packed = pack(columns)
    own, above, packed = lax.optimization_barrier((own, above, packed))
    pair = jnp.stack([own, above])
    far = [fetch(pair, dz=d) for d in (2, 4, 6)]
    line = jnp.concatenate([pair] + far)

    packed = exchange(packed, False)
    packed = exchange(jnp.swapaxes(packed, 0, 1), True)

    pieces, layout = [], []

    def keep(array, second, firsts):
        pieces.extend([array, fetch(array, swap=1)])
        layout.extend([(second, 0, firsts), (second, 1, firsts)])

    side = [fetch(line, first=d) for d in (1, 2, 3)]
    low, high = jnp.stack([line, side[0]]), jnp.stack(side[1:])
    keep(low, 0, 0)
    keep(high, 0, 2)
    ahead_low, behind_high = fetch(low, second=1), fetch(high, second=3)
    ahead_high, behind_low = fetch(high, second=1), fetch(low, second=3)
    ahead_low, vir_row = lax.optimization_barrier((ahead_low, eps_vir[None]))
    keep(ahead_low, 1, 0)
    keep(behind_high, 3, 2)
    keep(ahead_high, 1, 2)
    keep(behind_low, 3, 0)
    keep(fetch(ahead_low, second=1), 2, 0)
    keep(fetch(behind_high, second=3), 2, 2)

    return gamma(block_owner, round_order, eps_occ, vir_row, packed, pieces, tuple(layout))[None]


def solution(mesh):
    in_specs = (P(None, "slab", "occ"), P(), P(), P(), P())
    out_specs = P("occ", "slab", None)
    return jax.shard_map(
        on_device, mesh=mesh, in_specs=in_specs, out_specs=out_specs, check_vma=False
    )
```

```python
import functools

import jax
import jax.numpy as jnp
from jax import lax
from jax.experimental import pallas as pl
from jax.experimental.pallas import tpu as pltpu
from jax.sharding import PartitionSpec as P

ROUNDS = 2
NZ, NX, NY, NC = 8, 4, 4, 2
XY = 8
COLS = 64
ROWS = 160
TAIL = ROWS - 128
PACKED = COLS + COLS * TAIL // 128
GROUPS = 128 // TAIL
GROUP_COLS = COLS // GROUPS
BOTH = ("occ", "slab")
LINE = 2 * COLS + COLS // 2
VMEM_LIMIT = 20 * 1024 * 1024


def index(z, x, y, core):
    return ((z % NZ) * XY + (x % 2) * NY + y % NY) * 4 + (x % NX) // 2 * 2 + core


def fetch(block, dz=0, first=0, second=0, swap=0):
    pairs = []
    for z in range(NZ):
        for x in range(NX):
            for y in range(NY):
                for core in range(NC):
                    dx, dy = (first, second) if core else (second, first)
                    pairs.append((index(z + dz, x + dx, y + dy, core ^ swap), index(z, x, y, core)))
    return lax.ppermute(block, BOTH, pairs)


def position():
    occ, slab = lax.axis_index("occ"), lax.axis_index("slab")
    return lax.div(occ, XY), lax.div(slab, 2) * 2 + lax.rem(lax.div(occ, NY), 2), lax.rem(occ, NY), lax.rem(slab, 2)


def line_kernel(order, columns, out, rounds, sems):
    copies = [
        pltpu.make_async_copy(columns.at[order[k]], rounds.at[k], sems.at[k]) for k in range(ROUNDS)]
    for copy in copies:
        copy.start()
    for copy in copies:
        copy.wait()
    for k in range(ROUNDS):
        out[k * COLS:(k + 1) * COLS] = rounds[k, :, :128]
    half = COLS // 2
    tail = [rounds[k, h:h + half, 128:] for h in (0, half) for k in range(ROUNDS)]
    out[2 * COLS:] = jnp.concatenate(tail, axis=1)


def pack_line(columns, round_order):
    return pl.pallas_call(
        line_kernel,
        in_specs=[pl.BlockSpec(memory_space=pltpu.SMEM), pl.BlockSpec(memory_space=pltpu.HBM)],
        out_specs=pl.BlockSpec(memory_space=pltpu.VMEM),
        out_shape=jax.ShapeDtypeStruct((LINE, 128), jnp.bfloat16),
        scratch_shapes=[pltpu.VMEM((ROUNDS, COLS, ROWS), jnp.bfloat16), pltpu.SemaphoreType.DMA((ROUNDS,))],
    )(round_order, columns)


def pack_kernel(pieces, out):
    step = pieces.shape[0]
    for b in range(step):
        piece = pieces[b]
        z, spot = pl.program_id(0) * (step // XY) + b // XY, b % XY
        out[spot, z, :COLS] = piece[:, :128]
        tail = [piece[g * GROUP_COLS:(g + 1) * GROUP_COLS, 128:] for g in range(GROUPS)]
        out[spot, z, COLS:] = jnp.concatenate(tail, axis=1)


def pack(columns):
    blocks = columns.shape[0]
    step = 32
    return pl.pallas_call(
        pack_kernel,
        grid=(blocks // step,),
        in_specs=[pl.BlockSpec((step, COLS, ROWS), lambda i: (i, 0, 0))],
        out_specs=pl.BlockSpec((XY, NZ, PACKED, 128), lambda i: (0, 0, 0, 0)),
        out_shape=jax.ShapeDtypeStruct((XY, NZ, PACKED, 128), jnp.bfloat16),
        compiler_params=pltpu.CompilerParams(vmem_limit_bytes=VMEM_LIMIT),
    )(columns)


def exchange(packed, planes):
    groups = [[m * XY + o if planes else o * XY + m for m in range(8)] for o in range(8)]
    return lax.all_to_all(packed, "occ", split_axis=0, concat_axis=0, axis_index_groups=groups, tiled=True)


def gamma_kernel(layout, owner, order, eps_occ, eps_vir, packed, *refs):
    pieces, (out, weights, tails, block_ref, rows, right, amplitude, partial, result, load_sems, store_sem) = (
        refs[:len(layout)], refs[len(layout):])
    my_z, my_x, my_y, my_core = position()
    fetch_block = pltpu.make_async_copy(packed, block_ref, load_sems.at[NC])
    fetch_block.start()
    copies = [[], []]
    for swap in range(NC):
        for piece, (second, swapped, first) in zip(pieces, layout):
            if swapped == swap:
                place = weights.at[swap, second, pl.ds(first, piece.shape[0])]
                copies[swap].append(pltpu.make_async_copy(piece, place, load_sems.at[swap]))
    for copy in copies[0] + copies[1]:
        copy.start()

    def line_of(swap, x_hi, spot):
        core = 1 - my_core if swap else my_core
        dx = lax.rem(x_hi * 2 + spot // NY + NX - my_x, NX)
        dy = lax.rem(spot % NY + NY - my_y, NY)
        return weights.at[swap, jnp.where(core == 0, dx, dy), jnp.where(core == 0, dy, dx)]

    span = 4 * ROWS
    vir_blocks = eps_vir.shape[1] // span

    def energies(slot):
        block = owner[slot]
        start = pl.multiple_of(lax.rem(block, vir_blocks) * span, 128)
        return eps_occ[lax.div(block, vir_blocks)] - eps_vir[:, pl.ds(start, span)]

    mine = energies(lax.axis_index("occ"))
    left = mine[:, :ROWS]
    for s in range(1, 4):
        left = jnp.where(lax.axis_index("slab") == s, mine[:, s * ROWS:(s + 1) * ROWS], left)
    left = jnp.concatenate([left, jnp.zeros((1, 256 - ROWS), jnp.float32)], axis=1)
    left = jnp.broadcast_to(left, (256, 256)).T[:ROWS]
    theirs = [energies(order[k]) for k in range(ROUNDS)]
    for s in range(4):
        right[s] = jnp.concatenate([t[:, s * ROWS:s * ROWS + 128] for t in theirs], axis=1)
    right[4] = jnp.concatenate(
        [t[:, s * ROWS + 128:(s + 1) * ROWS] for s in range(4) for t in theirs], axis=1)

    plane_cols = XY * COLS
    fetch_block.wait()
    for dz in range(NZ):
        cols = slice(dz * plane_cols, (dz + 1) * plane_cols)
        block = block_ref[lax.rem(my_z + dz, NZ)]
        rows[:128, cols] = block[:, :COLS].reshape(plane_cols, 128).T
        tail = block[:, COLS:].astype(jnp.float32).reshape(XY * GROUP_COLS, 128)
        groups = [tail if g == 0 else pltpu.roll(tail, 128 - TAIL * g, 1) for g in range(GROUPS)]
        groups = [v.reshape(XY, 1, GROUP_COLS, 128) for v in groups]
        tail = jnp.concatenate(groups, axis=1).reshape(plane_cols, 128)
        rows[128:, cols] = tail.T[:TAIL].astype(jnp.bfloat16)

    def contract(p, pair):
        part = jnp.dot(rows[...], jnp.concatenate(pair, axis=1), preferred_element_type=jnp.float32)
        amplitude[p] = (part / (left + right[p])).astype(jnp.bfloat16)

    def slab_cols(lines, k, planes):
        return jnp.concatenate([v[z, k * COLS:(k + 1) * COLS] for z in planes for v in lines], axis=0)

    lines = [[line_of(swap, h, spot) for spot in range(XY)] for swap in range(NC) for h in range(2)]
    slabs = [2 * h + (1 - my_core if swap else my_core) for swap in range(NC) for h in range(2)] + [4]

    def turned(first, last):
        return jnp.concatenate([amplitude[p] for p in slabs[first:last]], axis=1).T

    for copy in copies[0]:
        copy.wait()
    for n in range(2):
        contract(slabs[n], [slab_cols(lines[n], k, range(NZ)) for k in range(ROUNDS)])
    by_slab = turned(0, 2)
    for dz in range(0, NZ, 2):
        planes = range(dz, dz + 2)
        part = [slab_cols(lines[n], k, planes) for n in range(2) for k in range(ROUNDS)]
        part = jnp.dot(jnp.concatenate(part, axis=1), by_slab, preferred_element_type=jnp.float32)
        partial[dz:dz + 2] = part.reshape(2, plane_cols, ROWS)

    for copy in copies[1]:
        copy.wait()
    for n in range(2, 4):
        contract(slabs[n], [slab_cols(lines[n], k, range(NZ)) for k in range(ROUNDS)])
    half = COLS // 2
    for h in range(2):
        for spot in range(XY):
            mine, other = line_of(0, h, spot), line_of(1, h, spot)
            for z in range(NZ):
                mine_tail, other_tail = mine[z, 2 * COLS:], other[z, 2 * COLS:]
                low = jnp.where(my_core == 0, mine_tail, other_tail)
                high = jnp.where(my_core == 0, other_tail, mine_tail)
                tails[h, z, spot, :half] = jnp.concatenate([low[:, :64], high[:, :64]], axis=1)
                tails[h, z, spot, half:] = jnp.concatenate([low[:, 64:], high[:, 64:]], axis=1)
    contract(4, [tails[h].reshape(NZ * plane_cols, 128) for h in range(2)])

    by_slab = turned(2, 5)
    stores = []
    for dz in range(0, NZ, 2):
        planes = range(dz, dz + 2)
        part = [slab_cols(lines[n], k, planes) for n in range(2, 4) for k in range(ROUNDS)]
        part += [tails[h, dz:dz + 2].reshape(2 * plane_cols, 128) for h in range(2)]
        part = jnp.dot(jnp.concatenate(part, axis=1), by_slab, preferred_element_type=jnp.float32)
        part = part.reshape(2, plane_cols, ROWS) + partial[dz:dz + 2]
        for z in planes:
            result[z] = part[z - dz].astype(jnp.bfloat16).T
            start = pl.multiple_of(lax.rem(my_z + z, NZ) * plane_cols, plane_cols)
            stores.append(pltpu.make_async_copy(result.at[z], out.at[:, pl.ds(start, plane_cols)], store_sem))
            stores[-1].start()
    for store in stores:
        store.wait()


def gamma(block_owner, round_order, eps_occ, vir_row, packed, pieces, layout):
    smem = pl.BlockSpec(memory_space=pltpu.SMEM)
    vmem = pl.BlockSpec(memory_space=pltpu.VMEM)
    return pl.pallas_call(
        functools.partial(gamma_kernel, layout),
        in_specs=[smem] * 3 + [vmem] + [pl.BlockSpec(memory_space=pl.ANY)] * (1 + len(pieces)),
        out_specs=pl.BlockSpec(memory_space=pltpu.HBM),
        out_shape=jax.ShapeDtypeStruct((ROWS, NZ * XY * COLS), jnp.bfloat16),
        scratch_shapes=[
            pltpu.VMEM((NC, 4, 4, NZ, LINE, 128), jnp.bfloat16),
            pltpu.VMEM((2, NZ, XY, COLS, 128), jnp.bfloat16),
            pltpu.VMEM((NZ, XY, PACKED, 128), jnp.bfloat16),
            pltpu.VMEM((ROWS, NZ * XY * COLS), jnp.bfloat16),
            pltpu.VMEM((5, 1, 256), jnp.float32),
            pltpu.VMEM((5, ROWS, 256), jnp.bfloat16),
            pltpu.VMEM((NZ, XY * COLS, ROWS), jnp.float32),
            pltpu.VMEM((NZ, ROWS, XY * COLS), jnp.bfloat16),
            pltpu.SemaphoreType.DMA((NC + 1,)),
            pltpu.SemaphoreType.DMA,
        ],
        compiler_params=pltpu.CompilerParams(vmem_limit_bytes=32 * 1024 * 1024),
    )(block_owner, round_order, eps_occ, vir_row, packed, *[pltpu.with_memory_space_constraint(v, pltpu.HBM) for v in pieces])


def on_device(three_centre, eps_occ, eps_vir, block_owner, round_order):
    columns = jnp.swapaxes(three_centre, 1, 2)

    own = pack_line(columns, round_order)
    above = fetch(own, dz=1)
    packed = pack(columns)
    own, above, packed = lax.optimization_barrier((own, above, packed))
    pair = jnp.stack([own, above])
    far = [fetch(pair, dz=d) for d in (2, 4, 6)]
    line = jnp.concatenate([pair] + far)

    packed = exchange(packed, False)
    packed = exchange(jnp.swapaxes(packed, 0, 1), True)

    pieces, layout = [], []

    def keep(array, second, firsts):
        pieces.extend([array, fetch(array, swap=1)])
        layout.extend([(second, 0, firsts), (second, 1, firsts)])

    side = [fetch(line, first=d) for d in (1, 2, 3)]
    low, high = jnp.stack([line, side[0]]), jnp.stack(side[1:])
    keep(low, 0, 0)
    keep(high, 0, 2)
    ahead_low, behind_high = fetch(low, second=1), fetch(high, second=3)
    ahead_high, behind_low = fetch(high, second=1), fetch(low, second=3)
    ahead_low, vir_row = lax.optimization_barrier((ahead_low, eps_vir[None]))
    keep(ahead_low, 1, 0)
    keep(behind_high, 3, 2)
    keep(ahead_high, 1, 2)
    keep(behind_low, 3, 0)
    keep(fetch(ahead_low, second=1), 2, 0)
    keep(fetch(behind_high, second=3), 2, 2)

    return gamma(block_owner, round_order, eps_occ, vir_row, packed, pieces, tuple(layout))[None]


def solution(mesh):
    in_specs = (P(None, "slab", "occ"), P(), P(), P(), P())
    out_specs = P("occ", "slab", None)
    return jax.shard_map(
        on_device, mesh=mesh, in_specs=in_specs, out_specs=out_specs, check_vma=False
    )
```

```python
import functools

import jax
import jax.numpy as jnp
from jax import lax
from jax.experimental import pallas as pl
from jax.experimental.pallas import tpu as pltpu
from jax.sharding import PartitionSpec as P

ROUNDS = 2
NZ, NX, NY, NC = 8, 4, 4, 2
XY = 8
COLS = 64
ROWS = 160
TAIL = ROWS - 128
PACKED = COLS + COLS * TAIL // 128
GROUPS = 128 // TAIL
GROUP_COLS = COLS // GROUPS
BOTH = ("occ", "slab")
LINE = 2 * COLS + COLS // 2
VMEM_LIMIT = 20 * 1024 * 1024


def index(z, x, y, core):
    return ((z % NZ) * XY + (x % 2) * NY + y % NY) * 4 + (x % NX) // 2 * 2 + core


def fetch(block, dz=0, first=0, second=0, swap=0):
    pairs = []
    for z in range(NZ):
        for x in range(NX):
            for y in range(NY):
                for core in range(NC):
                    dx, dy = (first, second) if core else (second, first)
                    pairs.append((index(z + dz, x + dx, y + dy, core ^ swap), index(z, x, y, core)))
    return lax.ppermute(block, BOTH, pairs)


def position():
    occ, slab = lax.axis_index("occ"), lax.axis_index("slab")
    return lax.div(occ, XY), lax.div(slab, 2) * 2 + lax.rem(lax.div(occ, NY), 2), lax.rem(occ, NY), lax.rem(slab, 2)


def line_kernel(order, columns, out, rounds, sems):
    copies = [
        pltpu.make_async_copy(columns.at[order[k]], rounds.at[k], sems.at[k]) for k in range(ROUNDS)]
    for copy in copies:
        copy.start()
    for copy in copies:
        copy.wait()
    for k in range(ROUNDS):
        out[k * COLS:(k + 1) * COLS] = rounds[k, :, :128]
    half = COLS // 2
    tail = [rounds[k, h:h + half, 128:] for h in (0, half) for k in range(ROUNDS)]
    out[2 * COLS:] = jnp.concatenate(tail, axis=1)


def pack_line(columns, round_order):
    return pl.pallas_call(
        line_kernel,
        in_specs=[pl.BlockSpec(memory_space=pltpu.SMEM), pl.BlockSpec(memory_space=pltpu.HBM)],
        out_specs=pl.BlockSpec(memory_space=pltpu.VMEM),
        out_shape=jax.ShapeDtypeStruct((LINE, 128), jnp.bfloat16),
        scratch_shapes=[pltpu.VMEM((ROUNDS, COLS, ROWS), jnp.bfloat16), pltpu.SemaphoreType.DMA((ROUNDS,))],
        compiler_params=pltpu.CompilerParams(vmem_limit_bytes=4 * 1024 * 1024),
    )(*[pltpu.with_memory_space_constraint(v, pltpu.HBM) for v in (round_order, columns)])


def pack_kernel(pieces, out):
    step = pieces.shape[0]
    for b in range(step):
        piece = pieces[b]
        z, spot = pl.program_id(0) * (step // XY) + b // XY, b % XY
        out[spot, z, :COLS] = piece[:, :128]
        tail = [piece[g * GROUP_COLS:(g + 1) * GROUP_COLS, 128:] for g in range(GROUPS)]
        out[spot, z, COLS:] = jnp.concatenate(tail, axis=1)


def pack(columns):
    blocks = columns.shape[0]
    step = 32
    return pl.pallas_call(
        pack_kernel,
        grid=(blocks // step,),
        in_specs=[pl.BlockSpec((step, COLS, ROWS), lambda i: (i, 0, 0))],
        out_specs=pl.BlockSpec((XY, NZ, PACKED, 128), lambda i: (0, 0, 0, 0)),
        out_shape=jax.ShapeDtypeStruct((XY, NZ, PACKED, 128), jnp.bfloat16),
        compiler_params=pltpu.CompilerParams(vmem_limit_bytes=VMEM_LIMIT),
    )(columns)


def exchange(packed, planes):
    groups = [[m * XY + o if planes else o * XY + m for m in range(8)] for o in range(8)]
    return lax.all_to_all(packed, "occ", split_axis=0, concat_axis=0, axis_index_groups=groups, tiled=True)


def gamma_kernel(layout, owner, order, eps_occ, eps_vir, packed, *refs):
    pieces, (out, weights, tails, block_ref, rows, right, amplitude, partial, result, load_sems, store_sem) = (
        refs[:len(layout)], refs[len(layout):])
    my_z, my_x, my_y, my_core = position()
    fetch_block = pltpu.make_async_copy(packed, block_ref, load_sems.at[NC])
    fetch_block.start()
    copies = [[], []]
    for swap in range(NC):
        for piece, (second, swapped, first) in zip(pieces, layout):
            if swapped == swap:
                place = weights.at[swap, second, pl.ds(first, piece.shape[0])]
                copies[swap].append(pltpu.make_async_copy(piece, place, load_sems.at[swap]))
    for copy in copies[0] + copies[1]:
        copy.start()

    def line_of(swap, x_hi, spot):
        core = 1 - my_core if swap else my_core
        dx = lax.rem(x_hi * 2 + spot // NY + NX - my_x, NX)
        dy = lax.rem(spot % NY + NY - my_y, NY)
        return weights.at[swap, jnp.where(core == 0, dx, dy), jnp.where(core == 0, dy, dx)]

    span = 4 * ROWS
    vir_blocks = eps_vir.shape[1] // span

    def energies(slot):
        block = owner[slot]
        start = pl.multiple_of(lax.rem(block, vir_blocks) * span, 128)
        return eps_occ[lax.div(block, vir_blocks)] - eps_vir[:, pl.ds(start, span)]

    mine = energies(lax.axis_index("occ"))
    left = mine[:, :ROWS]
    for s in range(1, 4):
        left = jnp.where(lax.axis_index("slab") == s, mine[:, s * ROWS:(s + 1) * ROWS], left)
    left = jnp.concatenate([left, jnp.zeros((1, 256 - ROWS), jnp.float32)], axis=1)
    left = jnp.broadcast_to(left, (256, 256)).T[:ROWS]
    theirs = [energies(order[k]) for k in range(ROUNDS)]
    for s in range(4):
        right[s] = jnp.concatenate([t[:, s * ROWS:s * ROWS + 128] for t in theirs], axis=1)
    right[4] = jnp.concatenate(
        [t[:, s * ROWS + 128:(s + 1) * ROWS] for s in range(4) for t in theirs], axis=1)

    plane_cols = XY * COLS
    fetch_block.wait()
    for dz in range(NZ):
        cols = slice(dz * plane_cols, (dz + 1) * plane_cols)
        block = block_ref[lax.rem(my_z + dz, NZ)]
        rows[:128, cols] = block[:, :COLS].reshape(plane_cols, 128).T
        tail = block[:, COLS:].astype(jnp.float32).reshape(XY * GROUP_COLS, 128)
        groups = [tail if g == 0 else pltpu.roll(tail, 128 - TAIL * g, 1) for g in range(GROUPS)]
        groups = [v.reshape(XY, 1, GROUP_COLS, 128) for v in groups]
        tail = jnp.concatenate(groups, axis=1).reshape(plane_cols, 128)
        rows[128:, cols] = tail.T[:TAIL].astype(jnp.bfloat16)

    def contract(p, pair):
        part = jnp.dot(rows[...], jnp.concatenate(pair, axis=1), preferred_element_type=jnp.float32)
        amplitude[p] = (part / (left + right[p])).astype(jnp.bfloat16)

    def slab_cols(lines, k, planes):
        return jnp.concatenate([v[z, k * COLS:(k + 1) * COLS] for z in planes for v in lines], axis=0)

    lines = [[line_of(swap, h, spot) for spot in range(XY)] for swap in range(NC) for h in range(2)]
    slabs = [2 * h + (1 - my_core if swap else my_core) for swap in range(NC) for h in range(2)] + [4]

    def turned(first, last):
        return jnp.concatenate([amplitude[p] for p in slabs[first:last]], axis=1).T

    for copy in copies[0]:
        copy.wait()
    for n in range(2):
        contract(slabs[n], [slab_cols(lines[n], k, range(NZ)) for k in range(ROUNDS)])
    by_slab = turned(0, 2)
    for dz in range(0, NZ, 2):
        planes = range(dz, dz + 2)
        part = [slab_cols(lines[n], k, planes) for n in range(2) for k in range(ROUNDS)]
        part = jnp.dot(jnp.concatenate(part, axis=1), by_slab, preferred_element_type=jnp.float32)
        partial[dz:dz + 2] = part.reshape(2, plane_cols, ROWS)

    for copy in copies[1]:
        copy.wait()
    for n in range(2, 4):
        contract(slabs[n], [slab_cols(lines[n], k, range(NZ)) for k in range(ROUNDS)])
    half = COLS // 2
    for h in range(2):
        for spot in range(XY):
            mine, other = line_of(0, h, spot), line_of(1, h, spot)
            for z in range(NZ):
                mine_tail, other_tail = mine[z, 2 * COLS:], other[z, 2 * COLS:]
                low = jnp.where(my_core == 0, mine_tail, other_tail)
                high = jnp.where(my_core == 0, other_tail, mine_tail)
                tails[h, z, spot, :half] = jnp.concatenate([low[:, :64], high[:, :64]], axis=1)
                tails[h, z, spot, half:] = jnp.concatenate([low[:, 64:], high[:, 64:]], axis=1)
    contract(4, [tails[h].reshape(NZ * plane_cols, 128) for h in range(2)])

    by_slab = turned(2, 5)
    stores = []
    for dz in range(0, NZ, 2):
        planes = range(dz, dz + 2)
        part = [slab_cols(lines[n], k, planes) for n in range(2, 4) for k in range(ROUNDS)]
        part += [tails[h, dz:dz + 2].reshape(2 * plane_cols, 128) for h in range(2)]
        part = jnp.dot(jnp.concatenate(part, axis=1), by_slab, preferred_element_type=jnp.float32)
        part = part.reshape(2, plane_cols, ROWS) + partial[dz:dz + 2]
        for z in planes:
            result[z] = part[z - dz].astype(jnp.bfloat16).T
            start = pl.multiple_of(lax.rem(my_z + z, NZ) * plane_cols, plane_cols)
            stores.append(pltpu.make_async_copy(result.at[z], out.at[:, pl.ds(start, plane_cols)], store_sem))
            stores[-1].start()
    for store in stores:
        store.wait()


def gamma(block_owner, round_order, eps_occ, vir_row, packed, pieces, layout):
    smem = pl.BlockSpec(memory_space=pltpu.SMEM)
    vmem = pl.BlockSpec(memory_space=pltpu.VMEM)
    return pl.pallas_call(
        functools.partial(gamma_kernel, layout),
        in_specs=[smem] * 3 + [vmem] + [pl.BlockSpec(memory_space=pl.ANY)] * (1 + len(pieces)),
        out_specs=pl.BlockSpec(memory_space=pltpu.HBM),
        out_shape=jax.ShapeDtypeStruct((ROWS, NZ * XY * COLS), jnp.bfloat16),
        scratch_shapes=[
            pltpu.VMEM((NC, 4, 4, NZ, LINE, 128), jnp.bfloat16),
            pltpu.VMEM((2, NZ, XY, COLS, 128), jnp.bfloat16),
            pltpu.VMEM((NZ, XY, PACKED, 128), jnp.bfloat16),
            pltpu.VMEM((ROWS, NZ * XY * COLS), jnp.bfloat16),
            pltpu.VMEM((5, 1, 256), jnp.float32),
            pltpu.VMEM((5, ROWS, 256), jnp.bfloat16),
            pltpu.VMEM((NZ, XY * COLS, ROWS), jnp.float32),
            pltpu.VMEM((NZ, ROWS, XY * COLS), jnp.bfloat16),
            pltpu.SemaphoreType.DMA((NC + 1,)),
            pltpu.SemaphoreType.DMA,
        ],
        compiler_params=pltpu.CompilerParams(vmem_limit_bytes=32 * 1024 * 1024),
    )(block_owner, round_order, eps_occ, vir_row, packed, *[pltpu.with_memory_space_constraint(v, pltpu.HBM) for v in pieces])


def on_device(three_centre, eps_occ, eps_vir, block_owner, round_order):
    columns = jnp.swapaxes(three_centre, 1, 2)

    own = pack_line(columns, round_order)
    above = fetch(own, dz=1)
    packed = pack(columns)
    own, above, packed = lax.optimization_barrier((own, above, packed))
    pair = jnp.stack([own, above])
    far = [fetch(pair, dz=d) for d in (2, 4, 6)]
    line = jnp.concatenate([pair] + far)

    packed = exchange(packed, False)
    packed = exchange(jnp.swapaxes(packed, 0, 1), True)

    pieces, layout = [], []

    def keep(array, second, firsts):
        pieces.extend([array, fetch(array, swap=1)])
        layout.extend([(second, 0, firsts), (second, 1, firsts)])

    side = [fetch(line, first=d) for d in (1, 2, 3)]
    low, high = jnp.stack([line, side[0]]), jnp.stack(side[1:])
    keep(low, 0, 0)
    keep(high, 0, 2)
    ahead_low, behind_high = fetch(low, second=1), fetch(high, second=3)
    ahead_high, behind_low = fetch(high, second=1), fetch(low, second=3)
    ahead_low, vir_row = lax.optimization_barrier((ahead_low, eps_vir[None]))
    keep(ahead_low, 1, 0)
    keep(behind_high, 3, 2)
    keep(ahead_high, 1, 2)
    keep(behind_low, 3, 0)
    keep(fetch(ahead_low, second=1), 2, 0)
    keep(fetch(behind_high, second=3), 2, 2)

    return gamma(block_owner, round_order, eps_occ, vir_row, packed, pieces, tuple(layout))[None]


def solution(mesh):
    in_specs = (P(None, "slab", "occ"), P(), P(), P(), P())
    out_specs = P("occ", "slab", None)
    return jax.shard_map(
        on_device, mesh=mesh, in_specs=in_specs, out_specs=out_specs, check_vma=False
    )
```

```python
import functools

import jax
import jax.numpy as jnp
from jax import lax
from jax.experimental import pallas as pl
from jax.experimental.pallas import tpu as pltpu
from jax.sharding import PartitionSpec as P

ROUNDS = 2
NZ, NX, NY, NC = 8, 4, 4, 2
XY = 8
COLS = 64
ROWS = 160
TAIL = ROWS - 128
PACKED = COLS + COLS * TAIL // 128
GROUPS = 128 // TAIL
GROUP_COLS = COLS // GROUPS
BOTH = ("occ", "slab")
LINE = 2 * COLS + COLS // 2
VMEM_LIMIT = 20 * 1024 * 1024


def index(z, x, y, core):
    return ((z % NZ) * XY + (x % 2) * NY + y % NY) * 4 + (x % NX) // 2 * 2 + core


def fetch(block, dz=0, first=0, second=0, swap=0):
    pairs = []
    for z in range(NZ):
        for x in range(NX):
            for y in range(NY):
                for core in range(NC):
                    dx, dy = (first, second) if core else (second, first)
                    pairs.append((index(z + dz, x + dx, y + dy, core ^ swap), index(z, x, y, core)))
    return lax.ppermute(block, BOTH, pairs)


def position():
    occ, slab = lax.axis_index("occ"), lax.axis_index("slab")
    return lax.div(occ, XY), lax.div(slab, 2) * 2 + lax.rem(lax.div(occ, NY), 2), lax.rem(occ, NY), lax.rem(slab, 2)


def line_kernel(order, columns, out, rounds, sems):
    copies = [
        pltpu.make_async_copy(columns.at[order[k]], rounds.at[k], sems.at[k]) for k in range(ROUNDS)]
    for copy in copies:
        copy.start()
    for copy in copies:
        copy.wait()
    for k in range(ROUNDS):
        out[k * COLS:(k + 1) * COLS] = rounds[k, :, :128]
    half = COLS // 2
    tail = [rounds[k, h:h + half, 128:] for h in (0, half) for k in range(ROUNDS)]
    out[2 * COLS:] = jnp.concatenate(tail, axis=1)


def pack_line(columns, round_order):
    return pl.pallas_call(
        line_kernel,
        in_specs=[pl.BlockSpec(memory_space=pltpu.SMEM), pl.BlockSpec(memory_space=pltpu.HBM)],
        out_specs=pl.BlockSpec(memory_space=pltpu.VMEM),
        out_shape=jax.ShapeDtypeStruct((LINE, 128), jnp.bfloat16),
        scratch_shapes=[pltpu.VMEM((ROUNDS, COLS, ROWS), jnp.bfloat16), pltpu.SemaphoreType.DMA((ROUNDS,))],
        compiler_params=pltpu.CompilerParams(vmem_limit_bytes=4 * 1024 * 1024),
    )(*[pltpu.with_memory_space_constraint(v, pltpu.HBM) for v in (round_order, columns)])


def pack_kernel(pieces, out):
    step = pieces.shape[0]
    for b in range(step):
        piece = pieces[b]
        z, spot = pl.program_id(0) * (step // XY) + b // XY, b % XY
        out[spot, z, :COLS] = piece[:, :128]
        tail = [piece[g * GROUP_COLS:(g + 1) * GROUP_COLS, 128:] for g in range(GROUPS)]
        out[spot, z, COLS:] = jnp.concatenate(tail, axis=1)


def pack(columns):
    blocks = columns.shape[0]
    step = 32
    return pl.pallas_call(
        pack_kernel,
        grid=(blocks // step,),
        in_specs=[pl.BlockSpec((step, COLS, ROWS), lambda i: (i, 0, 0))],
        out_specs=pl.BlockSpec((XY, NZ, PACKED, 128), lambda i: (0, 0, 0, 0)),
        out_shape=jax.ShapeDtypeStruct((XY, NZ, PACKED, 128), jnp.bfloat16),
        compiler_params=pltpu.CompilerParams(vmem_limit_bytes=VMEM_LIMIT),
    )(columns)


def exchange(packed, planes):
    groups = [[m * XY + o if planes else o * XY + m for m in range(8)] for o in range(8)]
    return lax.all_to_all(packed, "occ", split_axis=0, concat_axis=0, axis_index_groups=groups, tiled=True)


def gamma_kernel(layout, owner, order, eps_occ, eps_vir, packed, *refs):
    pieces, (out, weights, tails, block_ref, rows, right, amplitude, partial, result, load_sems, store_sem) = (
        refs[:len(layout)], refs[len(layout):])
    my_z, my_x, my_y, my_core = position()
    fetch_block = pltpu.make_async_copy(packed, block_ref, load_sems.at[NC])
    fetch_block.start()
    copies = [[], []]
    for swap in range(NC):
        for piece, (second, swapped, first) in zip(pieces, layout):
            if swapped == swap:
                place = weights.at[swap, second, pl.ds(first, piece.shape[0])]
                copies[swap].append(pltpu.make_async_copy(piece, place, load_sems.at[swap]))
    for copy in copies[0] + copies[1]:
        copy.start()

    def line_of(swap, x_hi, spot):
        core = 1 - my_core if swap else my_core
        dx = lax.rem(x_hi * 2 + spot // NY + NX - my_x, NX)
        dy = lax.rem(spot % NY + NY - my_y, NY)
        return weights.at[swap, jnp.where(core == 0, dx, dy), jnp.where(core == 0, dy, dx)]

    span = 4 * ROWS
    vir_blocks = eps_vir.shape[1] // span

    def energies(slot):
        block = owner[slot]
        start = pl.multiple_of(lax.rem(block, vir_blocks) * span, 128)
        return eps_occ[lax.div(block, vir_blocks)] - eps_vir[:, pl.ds(start, span)]

    mine = energies(lax.axis_index("occ"))
    left = mine[:, :ROWS]
    for s in range(1, 4):
        left = jnp.where(lax.axis_index("slab") == s, mine[:, s * ROWS:(s + 1) * ROWS], left)
    left = jnp.concatenate([left, jnp.zeros((1, 256 - ROWS), jnp.float32)], axis=1)
    left = jnp.broadcast_to(left, (256, 256)).T[:ROWS]
    theirs = [energies(order[k]) for k in range(ROUNDS)]
    for s in range(4):
        right[s] = jnp.concatenate([t[:, s * ROWS:s * ROWS + 128] for t in theirs], axis=1)
    right[4] = jnp.concatenate(
        [t[:, s * ROWS + 128:(s + 1) * ROWS] for s in range(4) for t in theirs], axis=1)

    plane_cols = XY * COLS
    fetch_block.wait()
    for dz in range(NZ):
        cols = slice(dz * plane_cols, (dz + 1) * plane_cols)
        block = block_ref[lax.rem(my_z + dz, NZ)]
        rows[:128, cols] = block[:, :COLS].reshape(plane_cols, 128).T
        tail = block[:, COLS:].astype(jnp.float32).reshape(XY * GROUP_COLS, 128)
        groups = [tail if g == 0 else pltpu.roll(tail, 128 - TAIL * g, 1) for g in range(GROUPS)]
        groups = [v.reshape(XY, 1, GROUP_COLS, 128) for v in groups]
        tail = jnp.concatenate(groups, axis=1).reshape(plane_cols, 128)
        rows[128:, cols] = tail.T[:TAIL].astype(jnp.bfloat16)

    def contract(p, pair):
        part = jnp.dot(rows[...], jnp.concatenate(pair, axis=1), preferred_element_type=jnp.float32)
        amplitude[p] = (part / (left + right[p])).astype(jnp.bfloat16)

    def slab_cols(lines, k, planes):
        return jnp.concatenate([v[z, k * COLS:(k + 1) * COLS] for z in planes for v in lines], axis=0)

    lines = [[line_of(swap, h, spot) for spot in range(XY)] for swap in range(NC) for h in range(2)]
    slabs = [2 * h + (1 - my_core if swap else my_core) for swap in range(NC) for h in range(2)] + [4]

    def turned(first, last):
        return jnp.concatenate([amplitude[p] for p in slabs[first:last]], axis=1).T

    for copy in copies[0]:
        copy.wait()
    for n in range(2):
        contract(slabs[n], [slab_cols(lines[n], k, range(NZ)) for k in range(ROUNDS)])
    by_slab = turned(0, 2)
    for dz in range(0, NZ, 2):
        planes = range(dz, dz + 2)
        part = [slab_cols(lines[n], k, planes) for n in range(2) for k in range(ROUNDS)]
        part = jnp.dot(jnp.concatenate(part, axis=1), by_slab, preferred_element_type=jnp.float32)
        partial[dz:dz + 2] = part.reshape(2, plane_cols, ROWS)

    for copy in copies[1]:
        copy.wait()
    for n in range(2, 4):
        contract(slabs[n], [slab_cols(lines[n], k, range(NZ)) for k in range(ROUNDS)])
    half = COLS // 2
    for h in range(2):
        for spot in range(XY):
            mine, other = line_of(0, h, spot), line_of(1, h, spot)
            for z in range(NZ):
                mine_tail, other_tail = mine[z, 2 * COLS:], other[z, 2 * COLS:]
                low = jnp.where(my_core == 0, mine_tail, other_tail)
                high = jnp.where(my_core == 0, other_tail, mine_tail)
                tails[h, z, spot, :half] = jnp.concatenate([low[:, :64], high[:, :64]], axis=1)
                tails[h, z, spot, half:] = jnp.concatenate([low[:, 64:], high[:, 64:]], axis=1)
    contract(4, [tails[h].reshape(NZ * plane_cols, 128) for h in range(2)])

    by_slab = turned(2, 5)
    stores = []
    for dz in range(0, NZ, 2):
        planes = range(dz, dz + 2)
        part = [slab_cols(lines[n], k, planes) for n in range(2, 4) for k in range(ROUNDS)]
        part += [tails[h, dz:dz + 2].reshape(2 * plane_cols, 128) for h in range(2)]
        part = jnp.dot(jnp.concatenate(part, axis=1), by_slab, preferred_element_type=jnp.float32)
        part = part.reshape(2, plane_cols, ROWS) + partial[dz:dz + 2]
        for z in planes:
            result[z] = part[z - dz].astype(jnp.bfloat16).T
            start = pl.multiple_of(lax.rem(my_z + z, NZ) * plane_cols, plane_cols)
            stores.append(pltpu.make_async_copy(result.at[z], out.at[:, pl.ds(start, plane_cols)], store_sem))
            stores[-1].start()
    for store in stores:
        store.wait()


def gamma(block_owner, round_order, eps_occ, vir_row, packed, pieces, layout):
    smem = pl.BlockSpec(memory_space=pltpu.SMEM)
    vmem = pl.BlockSpec(memory_space=pltpu.VMEM)
    return pl.pallas_call(
        functools.partial(gamma_kernel, layout),
        in_specs=[smem] * 3 + [vmem] + [pl.BlockSpec(memory_space=pl.ANY)] * (1 + len(pieces)),
        out_specs=pl.BlockSpec(memory_space=pltpu.HBM),
        out_shape=jax.ShapeDtypeStruct((ROWS, NZ * XY * COLS), jnp.bfloat16),
        scratch_shapes=[
            pltpu.VMEM((NC, 4, 4, NZ, LINE, 128), jnp.bfloat16),
            pltpu.VMEM((2, NZ, XY, COLS, 128), jnp.bfloat16),
            pltpu.VMEM((NZ, XY, PACKED, 128), jnp.bfloat16),
            pltpu.VMEM((ROWS, NZ * XY * COLS), jnp.bfloat16),
            pltpu.VMEM((5, 1, 256), jnp.float32),
            pltpu.VMEM((5, ROWS, 256), jnp.bfloat16),
            pltpu.VMEM((NZ, XY * COLS, ROWS), jnp.float32),
            pltpu.VMEM((NZ, ROWS, XY * COLS), jnp.bfloat16),
            pltpu.SemaphoreType.DMA((NC + 1,)),
            pltpu.SemaphoreType.DMA,
        ],
        compiler_params=pltpu.CompilerParams(vmem_limit_bytes=32 * 1024 * 1024),
    )(block_owner, round_order, eps_occ, vir_row, packed, *[pltpu.with_memory_space_constraint(v, pltpu.HBM) for v in pieces])


def on_device(three_centre, eps_occ, eps_vir, block_owner, round_order):
    columns = jnp.swapaxes(three_centre, 1, 2)

    own = pack_line(columns, round_order)
    above = fetch(own, dz=1)
    packed = pack(columns)
    own, above, packed = lax.optimization_barrier((own, above, packed))
    pair = jnp.stack([own, above])
    far = [fetch(pair, dz=d) for d in (2, 4, 6)]
    line = jnp.concatenate([pair] + far)

    packed = exchange(packed, False)
    packed = exchange(jnp.swapaxes(packed, 0, 1), True)

    pieces, layout = [], []

    def keep(array, second, firsts):
        pieces.extend([array, fetch(array, swap=1)])
        layout.extend([(second, 0, firsts), (second, 1, firsts)])

    side = [fetch(line, first=d) for d in (1, 2, 3)]
    low, high = jnp.stack([line, side[0]]), jnp.stack(side[1:])
    keep(low, 0, 0)
    keep(high, 0, 2)
    ahead_low, behind_high = fetch(low, second=1), fetch(high, second=3)
    ahead_high, behind_low = fetch(high, second=1), fetch(low, second=3)
    keep(ahead_low, 1, 0)
    keep(behind_high, 3, 2)
    keep(ahead_high, 1, 2)
    keep(behind_low, 3, 0)
    opposite, vir_row = lax.optimization_barrier((fetch(ahead_low, second=1), eps_vir[None]))
    keep(opposite, 2, 0)
    keep(fetch(behind_high, second=3), 2, 2)

    return gamma(block_owner, round_order, eps_occ, vir_row, packed, pieces, tuple(layout))[None]


def solution(mesh):
    in_specs = (P(None, "slab", "occ"), P(), P(), P(), P())
    out_specs = P("occ", "slab", None)
    return jax.shard_map(
        on_device, mesh=mesh, in_specs=in_specs, out_specs=out_specs, check_vma=False
    )
```
